512 devices in a mesh: blk: 32 (over x, y, core), uly: 16 (over z).
Axes of the slice: x: 4, y: 4, z: 16, core: 2. Of those that a mesh axis runs over, the one named last changes fastest.
Arguments:
- queries: bfloat16 [8192, 6144], P(('blk', 'uly')), may hold values from -120 to 120
- keys: bfloat16 [8192, 6144], P(('blk', 'uly')), may hold values from -6 to 6
- values: bfloat16 [8192, 6144], P(('blk', 'uly')), may hold values from -6 to 6
- window_mask: int32 [128, 27], P('blk'), may hold values from 0 to 1, as said below
- valid_count: int32 [128], P('blk'), may hold values from 2 to 64, as said below
Outputs:
- attended: bfloat16 [8192, 6144], P(('blk', 'uly'))
The draws below stay inside these ranges and needn't reach their ends.
Inputs may be any that keep to these rules, and one draw needn't show every extreme that they name: `window_mask`: entry o of a tile's row is 1 only if the tile at offset (o // 9 - 1, o // 3 % 3 - 1, o % 3 - 1) lies inside the grid; entry 13 (the tile itself) is always 1. `valid_count`: some tile has all 64 tokens live.
All inputs are finite; a program needn't handle non-finite values.
Results may differ from the reference program's by a relative error of at most 0.0033.
Values may be sent and summed in bfloat16 or wider, within the bound.
A program may use at most 64 MiB of HBM per device.

```python
import math
import jax
import jax.numpy as jnp
from jax import lax

HEADS = 48
HDIM = 128
TILE = 64
TFRAMES = 1
TH_DEV = 2
TW_DEV = 2
ROWB = 4
COLB = 8
TH = 8
TW = 16
TILES = 128
TOKENS = 8192


def base_keys(key):
    return jnp.clip(jax.random.normal(key, (TILES, TILE, HEADS * HDIM), jnp.float32), -6.0, 6.0)


def draw_keys(key, part):
    shared = base_keys(key)
    return shared.reshape(TOKENS, HEADS * HDIM).astype(jnp.bfloat16)


def draw_queries(key, part):
    key = jax.random.fold_in(key, 12)
    fresh_draw = 2.0 * jnp.clip(jax.random.normal(key, (TILES, TILE, HEADS * HDIM), jnp.float32), -6.0, 6.0)
    return fresh_draw.reshape(TOKENS, HEADS * HDIM).astype(jnp.bfloat16)


def draw_window_mask(key, part):
    key = jax.random.fold_in(key, 13)
    first_key, second_key = jax.random.split(key)
    tile_ids = jnp.arange(TILES, dtype=jnp.int32)
    block_tiles = TFRAMES * TH_DEV * TW_DEV
    block_ids = tile_ids // block_tiles
    inner_ids = tile_ids % block_tiles
    frame_pos = inner_ids // (TH_DEV * TW_DEV)
    row_pos = block_ids // COLB * TH_DEV + inner_ids // TW_DEV % TH_DEV
    column_pos = block_ids % COLB * TW_DEV + inner_ids % TW_DEV
    window_ids = jnp.arange(27, dtype=jnp.int32)
    frame_move = window_ids // 9 - 1
    row_move = window_ids // 3 % 3 - 1
    column_move = window_ids % 3 - 1
    frame_to = frame_pos[:, None] + frame_move[None, :]
    row_to = row_pos[:, None] + row_move[None, :]
    column_to = column_pos[:, None] + column_move[None, :]
    inside = (frame_to >= 0) & (frame_to < TFRAMES) & (row_to >= 0) & (row_to < TH) & (column_to >= 0) & (column_to < TW)
    keep_share = jax.random.randint(first_key, (TILES, 1), 30, 101)
    dice_roll = jax.random.randint(second_key, (TILES, 27), 0, 100)
    picked = (dice_roll < keep_share) & inside | (window_ids == 13)[None, :]
    return picked.astype(jnp.int32)


def draw_valid_count(key, part):
    key = jax.random.fold_in(key, 14)
    drawn = jax.random.randint(key, (TILES,), 2, 2 * TILE + 1)
    capped = jnp.minimum(drawn, TILE)
    return capped.at[0].set(TILE).astype(jnp.int32)


def shard_levels(own_key, dims, cuts, least, top_value):
    level, own = 1.0, jax.random.fold_in(own_key, 6)
    for axis_at, blocks in cuts:
        steps = jnp.exp(jax.random.uniform(jax.random.fold_in(own, axis_at), (blocks,), jnp.float32, least / len(cuts), top_value / len(cuts)))
        level = level * jnp.repeat(steps, dims[axis_at] // blocks).reshape([-1 if axis == axis_at else 1 for axis in range(len(dims))])
    return level


def centred(own_key, dims, width, bound, cuts=(), kind=jnp.bfloat16):
    gain = shard_levels(own_key, dims, cuts, -0.22, 0.18) if cuts else 1.0
    values = jax.random.normal(own_key, dims, jnp.float32) * width * gain
    return jnp.minimum(jnp.maximum(values, -bound), bound).astype(kind)


def setup_inputs(seed: int = 0) -> dict:
    key_of = jax.random.split(jax.random.key(seed), 6)
    return {
        "queries": draw_queries(jax.random.fold_in(key_of[5], 71), 0),
        "keys": draw_keys(jax.random.fold_in(key_of[5], 71), 0),
        "values": centred(key_of[2], (TOKENS, HEADS * HDIM), 1.0, 6.0, ((0, 512),)),
        "window_mask": draw_window_mask(jax.random.fold_in(key_of[5], 71), 0),
        "valid_count": draw_valid_count(jax.random.fold_in(key_of[5], 71), 0),
    }


def to_grid(block_rows):
    rest = block_rows.shape[1:]
    shaped = block_rows.reshape((ROWB, COLB, TFRAMES, TH_DEV, TW_DEV) + rest)
    order = (2, 0, 3, 1, 4) + tuple(range(5, 5 + len(rest)))
    return jnp.transpose(shaped, order).reshape((TFRAMES, TH, TW) + rest)

def from_grid(grid):
    rest = grid.shape[3:]
    shaped = grid.reshape((TFRAMES, ROWB, TH_DEV, COLB, TW_DEV) + rest)
    order = (1, 3, 0, 2, 4) + tuple(range(5, 5 + len(rest)))
    return jnp.transpose(shaped, order).reshape((TILES,) + rest)

def reference(queries, keys, values, window_mask, valid_count):
    score_scale = 1.0 / math.sqrt(HDIM)
    tile_grid = (TFRAMES, TH, TW, TILE, HDIM)
    window_live = to_grid(window_mask)
    count_pad = jnp.pad(to_grid(valid_count), 1)
    positions = jnp.arange(TILE, dtype=jnp.int32)
    live_blocks = []
    for window_offset in range(27):
        frame_step, row_step, column_step = (window_offset // 9, window_offset // 3 % 3, window_offset % 3)
        count_tiles = count_pad[frame_step:frame_step + TFRAMES, row_step:row_step + TH, column_step:column_step + TW]
        live_blocks.append((positions[None, None, None, :] < count_tiles[..., None]) & (window_live[..., window_offset:window_offset + 1] > 0))
    spacing = ((1, 1), (1, 1), (1, 1), (0, 0), (0, 0))

    def head_grid(source, col_start):
        columns = lax.dynamic_slice_in_dim(source, col_start, HDIM, 1).astype(jnp.float32)
        return to_grid(columns.reshape(TILES, TILE, HDIM))

    def one_head(head_index):
        col_start = head_index * HDIM
        q_head = head_grid(queries, col_start)
        k_head = jnp.pad(head_grid(keys, col_start), spacing)
        v_head = jnp.pad(head_grid(values, col_start), spacing)

        def window_slice(source, window_offset):
            frame_step, row_step, column_step = (window_offset // 9, window_offset // 3 % 3, window_offset % 3)
            return source[frame_step:frame_step + TFRAMES, row_step:row_step + TH, column_step:column_step + TW]

        def scores_at(window_offset):
            raw_scores = jnp.einsum('fabqd,fabkd->fabqk', q_head, window_slice(k_head, window_offset), precision=lax.Precision.HIGHEST) * score_scale
            return jnp.where(live_blocks[window_offset][:, :, :, None, :], raw_scores, -1e+30)
        row_peak = jnp.full((TFRAMES, TH, TW, TILE), -1e+30, jnp.float32)
        for window_offset in range(27):
            row_peak = jnp.maximum(row_peak, lax.optimization_barrier(jnp.max(scores_at(window_offset), axis=-1)))
        row_total = jnp.zeros((TFRAMES, TH, TW, TILE), jnp.float32)
        summed = jnp.zeros(tile_grid, jnp.float32)
        for window_offset in range(27):
            exp_terms = jnp.where(live_blocks[window_offset][:, :, :, None, :], jnp.exp(scores_at(window_offset) - row_peak[..., None]), 0.0)
            row_total = row_total + lax.optimization_barrier(jnp.sum(exp_terms, axis=-1))
            weights = lax.optimization_barrier(exp_terms.astype(jnp.bfloat16)).astype(jnp.float32)
            summed = summed + jnp.einsum('fabqk,fabkd->fabqd', weights, window_slice(v_head, window_offset), precision=lax.Precision.HIGHEST)
        result = (summed / row_total[..., None]).astype(jnp.bfloat16)
        return from_grid(result).reshape(TOKENS, HDIM)
    per_head = lax.map(one_head, jnp.arange(HEADS, dtype=jnp.int32))
    return jnp.transpose(per_head, (1, 0, 2)).reshape(TOKENS, HEADS * HDIM)
```

```python
import functools
import math

import jax
import jax.numpy as jnp
from jax import lax
from jax.experimental import pallas as pl
from jax.experimental.pallas import tpu as pltpu
from jax.sharding import PartitionSpec as P

HDIM = 128
TILE = 64
ROWB, COLB = 4, 8
ULY = 16
PART = 16
LOCAL_HEADS = 3
NEG = -1e30
EXP_SCALE = math.log2(math.e) / math.sqrt(HDIM)
MOVES = [(a, b) for a in (-1, 0, 1) for b in (-1, 0, 1)]


def near(move):
    return pl.ds(1, 2) if move == 0 else pl.ds(2, 1) if move == 1 else pl.ds(1, 1)


def far(move):
    return pl.ds(1, 2) if move == 0 else pl.ds(0, 1) if move == 1 else pl.ds(3, 1)


def wait_bytes(ref, sem):
    pltpu.make_async_copy(ref, ref, sem).wait()


def kernel(count_s, mask_s, q_in, k_in, v_in, out, kv, qb, ob, cnt, bias,
           own_sem, send_sem, halo_send, cnt_send, out_send, out_own,
           in_recv, halo_recv, cnt_recv, out_recv):
    blk = lax.axis_index("blk")
    z = lax.axis_index("uly")
    row, col = blk // COLB, blk % COLB

    def neighbour(a, b):
        return lax.rem(row + a + ROWB, ROWB) * COLB + lax.rem(col + b + COLB, COLB)

    others = [m for m in MOVES if m != (0, 0)]
    barrier = pltpu.get_barrier_semaphore()

    def greet(d, carry):
        pl.semaphore_signal(barrier, inc=1, device_id=(blk, lax.rem(z + d, ULY)),
                            device_id_type=pl.DeviceIdType.MESH)
        return carry

    lax.fori_loop(1, ULY, greet, 0)
    for a, b in others:
        pl.semaphore_signal(barrier, inc=1, device_id=(neighbour(a, b), z),
                            device_id_type=pl.DeviceIdType.MESH)

    def columns(peer, head):
        return pl.ds(pl.multiple_of((peer * LOCAL_HEADS + head) * HDIM, HDIM), HDIM)

    def slot(array, head, part):
        rows = pl.ds(pl.multiple_of(lax.rem(part, 4) * PART, PART), PART)
        if array == 2:
            return qb.at[head, pl.ds(pl.multiple_of(part * PART, PART), PART)]
        return kv.at[head, array, 1 + part // 8, 1 + lax.rem(part // 4, 2), rows]

    sources = (k_in, v_in, q_in)

    own = []
    for head in range(LOCAL_HEADS):
        for array in range(3):
            copy = pltpu.make_async_copy(sources[array].at[:, columns(z, head)],
                                         slot(array, head, z), own_sem.at[head, array])
            copy.start()
            own.append(copy)

    for tile in range(4):
        cnt[4, tile:tile + 1, :] = jnp.full((1, 128), count_s[tile], jnp.int32)
    for tile in range(4):
        cnt[4, tile + 4:tile + 5, :] = jnp.zeros((1, 128), jnp.int32)

    pl.semaphore_wait(barrier, ULY - 1 + len(others))

    def ring(step):
        return 8 + (step + 1) // 2 * (2 * lax.rem(step, 2) - 1)

    def scatter(array, head):
        def body(step, carry):
            peer = lax.rem(z + ring(step), ULY)
            pltpu.make_async_remote_copy(
                src_ref=sources[array].at[:, columns(peer, head)],
                dst_ref=slot(array, head, z),
                send_sem=send_sem.at[array],
                recv_sem=in_recv.at[head, array],
                device_id=(blk, peer),
                device_id_type=pl.DeviceIdType.MESH,
            ).start()
            return carry

        lax.fori_loop(0, ULY - 1, body, 0)

    def arrived(array, head):
        own[head * 3 + array].wait()
        wait_bytes(qb.at[head, pl.ds(0, (ULY - 1) * PART)], in_recv.at[head, array])

    def halo(array, head):
        for a, b in others:
            pltpu.make_async_remote_copy(
                src_ref=kv.at[head, array, near(a), near(b)],
                dst_ref=kv.at[head, array, far(a), far(b)],
                send_sem=halo_send,
                recv_sem=halo_recv.at[head, array],
                device_id=(neighbour(a, b), z),
                device_id_type=pl.DeviceIdType.MESH,
            ).start()

    def halo_arrived(array, head):
        wait_bytes(kv.at[head, array, pl.ds(0, 3)], halo_recv.at[head, array])

    scatter(0, 0)
    scatter(1, 0)
    for index, (a, b) in enumerate(MOVES):
        if (a, b) != (0, 0):
            pltpu.make_async_remote_copy(
                src_ref=cnt.at[4],
                dst_ref=cnt.at[8 - index],
                send_sem=cnt_send,
                recv_sem=cnt_recv,
                device_id=(neighbour(a, b), z),
                device_id_type=pl.DeviceIdType.MESH,
            ).start()
    scatter(2, 0)
    scatter(0, 1)
    scatter(1, 1)

    def build_bias():
        wait_bytes(cnt.at[pl.ds(0, 8)], cnt_recv)
        lane = lax.broadcasted_iota(jnp.int32, (1, 128), 1)
        low = lane < TILE
        place = lax.rem(lane, TILE)

        def tile_count(r, c):
            a, b = (r + 1) // 2 - 1, (c + 1) // 2 - 1
            tile = (r + 1) % 2 * 2 + (c + 1) % 2
            return cnt[(a + 1) * 3 + b + 1, tile:tile + 1, :]

        for r in range(4):
            for half in range(2):
                live = place < jnp.where(low, tile_count(r, 2 * half), tile_count(r, 2 * half + 1))
                for tile in range(4):
                    qr, qc = tile // 2, tile % 2
                    kr = r - qr
                    if not 0 <= kr < 3:
                        continue
                    picks = []
                    for c in (2 * half, 2 * half + 1):
                        e = c - qc
                        picks.append(mask_s[tile, 9 + 3 * kr + e] if 0 <= e < 3 else 0)
                    picked = jnp.where(low, picks[0], picks[1])
                    start = kr * 256 + half * 128
                    bias[tile:tile + 1, start:start + 128] = jnp.where(
                        live & (picked > 0), 0.0, NEG).astype(jnp.float32)

    def compute(head):
        for qr in range(2):
            q = qb[head, qr * 128:(qr + 1) * 128, :]
            k = kv[head, 0, qr:qr + 3].reshape(768, HDIM)
            v = kv[head, 1, qr:qr + 3].reshape(768, HDIM)
            raw = lax.dot_general(q, k, (((1,), (1,)), ((), ())),
                                  preferred_element_type=jnp.float32)
            raw = (raw.reshape(2, TILE, 768) + bias[2 * qr:2 * qr + 2, :].reshape(2, 1, 768)).reshape(128, 768)
            peak = jnp.max(raw, axis=1, keepdims=True)
            expo = jnp.exp2((raw - peak) * EXP_SCALE)
            total = jnp.sum(expo, axis=1, keepdims=True)
            summed = jnp.dot(expo.astype(jnp.bfloat16), v, preferred_element_type=jnp.float32)
            ob[head, qr * 128:(qr + 1) * 128, :] = (summed / total).astype(jnp.bfloat16)

    def gather(head):
        def body(step, carry):
            peer = lax.rem(z + ring(step), ULY)
            pltpu.make_async_remote_copy(
                src_ref=ob.at[head, pl.ds(pl.multiple_of(peer * PART, PART), PART)],
                dst_ref=out.at[:, columns(z, head)],
                send_sem=out_send,
                recv_sem=out_recv,
                device_id=(blk, peer),
                device_id_type=pl.DeviceIdType.MESH,
            ).start()
            return carry

        lax.fori_loop(0, ULY - 1, body, 0)
        copy = pltpu.make_async_copy(
            ob.at[head, pl.ds(pl.multiple_of(z * PART, PART), PART)],
            out.at[:, columns(z, head)], out_own.at[head])
        copy.start()
        return copy

    last = []
    for head in range(LOCAL_HEADS):
        arrived(0, head)
        halo(0, head)
        arrived(1, head)
        halo(1, head)
        if head + 1 < LOCAL_HEADS:
            scatter(2, head + 1)
        if head == 0:
            scatter(0, 2)
            scatter(1, 2)
            build_bias()
        arrived(2, head)
        halo_arrived(0, head)
        halo_arrived(1, head)
        compute(head)
        last.append(gather(head))

    sent = pl.ds(0, LOCAL_HEADS * (ULY - 1) * HDIM)
    for array in range(3):
        wait_bytes(sources[array].at[:, sent], send_sem.at[array])
    for head in range(LOCAL_HEADS):
        for array in range(2):
            wait_bytes(kv.at[head, array, pl.ds(0, 3)], halo_send)
    wait_bytes(cnt.at[pl.ds(0, 8)], cnt_send)
    for copy in last:
        copy.wait()
    wait_bytes(out.at[:, sent], out_send)
    wait_bytes(out.at[:, sent], out_recv)


def on_device(queries, keys, values, window_mask, valid_count):
    heads = LOCAL_HEADS
    dma = pltpu.SemaphoreType.DMA
    return pl.pallas_call(
        kernel,
        out_shape=jax.ShapeDtypeStruct(queries.shape, queries.dtype),
        in_specs=[pl.BlockSpec(memory_space=pltpu.SMEM)] * 2 + [pl.BlockSpec(memory_space=pl.ANY)] * 3,
        out_specs=pl.BlockSpec(memory_space=pl.ANY),
        scratch_shapes=[
            pltpu.VMEM((heads, 2, 4, 4, TILE, HDIM), jnp.bfloat16),
            pltpu.VMEM((heads, 256, HDIM), jnp.bfloat16),
            pltpu.VMEM((heads, 256, HDIM), jnp.bfloat16),
            pltpu.VMEM((9, 8, 128), jnp.int32),
            pltpu.VMEM((8, 768), jnp.float32),
            dma((heads, 3)), dma((3,)), dma, dma, dma, dma((heads,)),
            dma((heads, 3)), dma((heads, 2)), dma, dma,
        ],
        compiler_params=pltpu.CompilerParams(
            collective_id=0, has_side_effects=True, vmem_limit_bytes=24 * 1024 * 1024),
    )(valid_count, window_mask, queries, keys, values)


def solution(mesh):
    in_specs = (
        P(("blk", "uly"), None),
        P(("blk", "uly"), None),
        P(("blk", "uly"), None),
        P("blk", None),
        P("blk"),
    )
    out_specs = P(("blk", "uly"), None)
    return jax.shard_map(
        on_device, mesh=mesh, in_specs=in_specs, out_specs=out_specs, check_vma=False
    )
```

```python
import math

import jax
import jax.numpy as jnp
from jax import lax
from jax.experimental import pallas as pl
from jax.experimental.pallas import tpu as pltpu
from jax.sharding import PartitionSpec as P

HDIM = 128
TILE = 64
ROWB, COLB = 4, 8
ULY = 16
HALF = ULY // 2
PART = 16
LOCAL_HEADS = 3
NEG = -1e30
EXP_SCALE = math.log2(math.e) / math.sqrt(HDIM)
MOVES = [(a, b) for a in (-1, 0, 1) for b in (-1, 0, 1)]
MESH = pl.DeviceIdType.MESH

ALL, FAR, NEAR = (0, ULY - 1), (0, 7), (7, ULY - 1)
SCHEDULE = (
    ('k', 0, ALL),
    ('v', 0, ALL),
    ('counts', 0),
    ('q', 0, ALL),
    ('k', 1, ALL),
    ('v', 1, ALL),
    ('k', 2, ALL),
    ('v', 2, ALL),
    ('q', 1, FAR),
    ('q', 2, FAR),
    ('q', 1, NEAR),
    ('q', 2, NEAR),
    ('hk', 0),
    ('hv', 0),
    ('bias', 0),
    ('hk', 1),
    ('hv', 1),
    ('c', 0, 0),
    ('c', 0, 1),
    ('o', 0, ALL, 2),
    ('hk', 2),
    ('hv', 2),
    ('c', 1, 0),
    ('o', 1, FAR, 0),
    ('c', 1, 1),
    ('o', 1, FAR, 1),
    ('c', 2, 0),
    ('o', 2, FAR, 0),
    ('c', 2, 1),
    ('o', 2, FAR, 1),
    ('o', 1, NEAR, 2),
    ('o', 2, NEAR, 2),
)


def near(move):
    return pl.ds(1, 2) if move == 0 else pl.ds(2, 1) if move == 1 else pl.ds(1, 1)


def far(move):
    return pl.ds(1, 2) if move == 0 else pl.ds(0, 1) if move == 1 else pl.ds(3, 1)


def wait_bytes(ref, sem):
    pltpu.make_async_copy(ref, ref, sem).wait()


def kernel(count_in, mask_in, q_in, k_in, v_in, out, kv, qb, ob, cnt, bias, count_s, mask_s,
           small, send_sem, halo_send, cnt_send, out_send,
           kv_recv, q_recv, halo_recv, cnt_recv, out_recv):
    blk = lax.axis_index("blk")
    z = lax.axis_index("uly")
    half = z // HALF
    row, col = blk // COLB, blk % COLB

    up, down = row > 0, row < ROWB - 1
    left, right = col > 0, col < COLB - 1
    others = sorted((m for m in MOVES if m != (0, 0)), key=lambda m: -abs(m[0]) - abs(m[1]))
    barrier = pltpu.get_barrier_semaphore()
    cnt[...] = jnp.zeros_like(cnt)

    def to_neighbour(a, b):
        return (blk + a * COLB + b, z)

    def if_inside(a, b):
        inside = [have for have, wanted in ((up, a < 0), (down, a > 0), (left, b < 0), (right, b > 0)) if wanted]
        return pl.when(inside[0] if len(inside) == 1 else inside[0] & inside[1])

    def ring(step):
        return 8 + (step + 1) // 2 * (2 * lax.rem(step, 2) - 1)

    def greet(d, carry):
        pl.semaphore_signal(barrier, inc=1, device_id=(blk, lax.rem(z + ring(d), ULY)), device_id_type=MESH)
        return carry

    lax.fori_loop(0, ULY - 1, greet, 0)
    for a, b in others:
        @if_inside(a, b)
        def _():
            pl.semaphore_signal(barrier, inc=1, device_id=to_neighbour(a, b), device_id_type=MESH)

    def columns(peer, head):
        return pl.ds(pl.multiple_of((peer * LOCAL_HEADS + head) * HDIM, HDIM), HDIM)

    def rows_of(part):
        return pl.ds(pl.multiple_of(part * PART, PART), PART)

    def kv_slot(array, head, part):
        return kv.at[head, array, 1 + part // HALF, 1 + lax.rem(part // 4, 2), rows_of(lax.rem(part, 4))]

    kv_in = (k_in, v_in)

    loads = [pltpu.make_async_copy(count_in, count_s, small.at[0]),
             pltpu.make_async_copy(mask_in, mask_s, small.at[1])]
    for copy in loads:
        copy.start()
    for head in range(LOCAL_HEADS):
        for array in range(2):
            pltpu.make_async_copy(kv_in[array].at[:, columns(z, head)], kv_slot(array, head, z),
                                  kv_recv.at[head, array]).start()
        pltpu.make_async_copy(q_in.at[:, columns(z, head)], qb.at[head, rows_of(z)],
                              q_recv.at[head]).start()

    for edge, at in ((~up, 0), (~down, 3)):
        @pl.when(edge)
        def _():
            kv[:, :, at:at + 1] = jnp.zeros((LOCAL_HEADS, 2, 1, 4, TILE, HDIM), kv.dtype)
    for edge, at in ((~left, 0), (~right, 3)):
        @pl.when(edge)
        def _():
            kv[:, :, :, at:at + 1] = jnp.zeros((LOCAL_HEADS, 2, 4, 1, TILE, HDIM), kv.dtype)

    across = 1 + left.astype(jnp.int32) + right.astype(jnp.int32)
    along = 1 + up.astype(jnp.int32) + down.astype(jnp.int32)
    pl.semaphore_wait(barrier, ULY - 2 + across * along)

    def scatter(array, head, steps):
        def body(step, carry):
            peer = lax.rem(z + ring(step), ULY)
            pltpu.make_async_remote_copy(
                src_ref=kv_in[array].at[:, columns(peer, head)],
                dst_ref=kv_slot(array, head, z),
                send_sem=send_sem.at[array],
                recv_sem=kv_recv.at[head, array],
                device_id=(blk, peer),
                device_id_type=MESH,
            ).start()
            return carry

        lax.fori_loop(*steps, body, 0)

    def scatter_queries(head, steps):
        def body(step, carry):
            peer = lax.rem(z + ring(step), ULY)
            pltpu.make_async_remote_copy(
                src_ref=q_in.at[:, columns(peer, head)],
                dst_ref=qb.at[head, rows_of(z)],
                send_sem=send_sem.at[2],
                recv_sem=q_recv.at[head],
                device_id=(blk, peer),
                device_id_type=MESH,
            ).start()
            return carry

        lax.fori_loop(*steps, body, 0)

    def send_counts():
        for copy in loads:
            copy.wait()
        for tile in range(8):
            cnt[4, tile:tile + 1, :] = jnp.full((1, 128), count_s[tile % 4], jnp.int32)
        for a, b in others:
            @if_inside(a, b)
            def _():
                index = (a + 1) * 3 + b + 1
                pltpu.make_async_remote_copy(
                    src_ref=cnt.at[4],
                    dst_ref=cnt.at[8 - index],
                    send_sem=cnt_send.at[index],
                    recv_sem=cnt_recv.at[index],
                    device_id=to_neighbour(a, b),
                    device_id_type=MESH,
                ).start()

    def halo(array, head):
        wait_bytes(qb.at[head], kv_recv.at[head, array])
        for a, b in others:
            @if_inside(a, b)
            def _():
                index = (a + 1) * 3 + b + 1
                pltpu.make_async_remote_copy(
                    src_ref=kv.at[head, array, near(a), near(b)],
                    dst_ref=kv.at[head, array, far(a), far(b)],
                    send_sem=halo_send.at[index],
                    recv_sem=halo_recv.at[head, array, index],
                    device_id=to_neighbour(a, b),
                    device_id_type=MESH,
                ).start()

    def halo_arrived(array, head):
        for a, b in others:
            @if_inside(a, b)
            def _():
                wait_bytes(kv.at[head, array, far(-a), far(-b)],
                           halo_recv.at[head, array, (1 - a) * 3 + 1 - b])

    def build_bias():
        for a, b in others:
            @if_inside(a, b)
            def _():
                wait_bytes(cnt.at[0], cnt_recv.at[(1 - a) * 3 + 1 - b])
        lane = lax.broadcasted_iota(jnp.int32, (1, 128), 1)
        low = lane < TILE
        place = lax.rem(lane, TILE)

        def tile_count(r, c):
            a, b = (r + 1) // 2 - 1, (c + 1) // 2 - 1
            tile = (r + 1) % 2 * 2 + (c + 1) % 2
            return cnt[(a + 1) * 3 + b + 1, tile:tile + 1, :]

        for r in range(4):
            for pair in range(2):
                live = place < jnp.where(low, tile_count(r, 2 * pair), tile_count(r, 2 * pair + 1))
                for tile in range(4):
                    qr, qc = tile // 2, tile % 2
                    kr = r - qr
                    if not 0 <= kr < 3:
                        continue
                    picks = []
                    for c in (2 * pair, 2 * pair + 1):
                        e = c - qc
                        picks.append(mask_s[tile, 9 + 3 * kr + e] if 0 <= e < 3 else 0)
                    picked = jnp.where(low, picks[0], picks[1])
                    start = kr * 256 + pair * 128
                    bias[qr, qc:qc + 1, start:start + 128] = jnp.where(
                        live & (picked > 0), 0.0, NEG).astype(jnp.float32)

    def compute(head, qr):
        rows = pl.ds(pl.multiple_of(qr * 128, 128), 128)
        k = kv[head, 0, pl.ds(qr, 3)].reshape(768, HDIM)
        v = kv[head, 1, pl.ds(qr, 3)].reshape(768, HDIM)
        raw = lax.dot_general(qb[head, rows, :], k, (((1,), (1,)), ((), ())),
                              preferred_element_type=jnp.float32)
        raw = (raw.reshape(2, TILE, 768) + bias[qr].reshape(2, 1, 768)).reshape(128, 768)
        peak = jnp.max(raw, axis=1, keepdims=True)
        expo = jnp.exp2((raw - peak) * EXP_SCALE)
        total = jnp.sum(expo, axis=1, keepdims=True)
        summed = jnp.dot(expo.astype(jnp.bfloat16), v, preferred_element_type=jnp.float32)
        ob[head, rows, :] = (summed / total).astype(jnp.bfloat16)

    def give_back(head, steps, which):
        def body(step, carry):
            peer = lax.rem(z + ring(step), ULY)

            def send():
                pltpu.make_async_remote_copy(
                    src_ref=ob.at[head, rows_of(peer)],
                    dst_ref=out.at[:, columns(z, head)],
                    send_sem=out_send,
                    recv_sem=out_recv,
                    device_id=(blk, peer),
                    device_id_type=MESH,
                ).start()

            if which == 2:
                send()
            else:
                pl.when((peer // HALF == half) == (which == 1))(send)
            return carry

        lax.fori_loop(*steps, body, 0)

    complete = set()
    for step in SCHEDULE:
        op, head, *rest = step
        if op in ("k", "v"):
            scatter("kv".index(op), head, *rest)
        elif op == "q":
            scatter_queries(head, *rest)
        elif op in ("hk", "hv"):
            halo("kv".index(op[1]), head)
        elif op == "counts":
            send_counts()
        elif op == "bias":
            build_bias()
        elif op == "c":
            if head not in complete:
                complete.add(head)
                halo_arrived(0, head)
                halo_arrived(1, head)
                wait_bytes(qb.at[head], q_recv.at[head])
            if rest[0] == 0:
                compute(head, 1 - half)
            else:
                compute(head, half)
                pltpu.make_async_copy(ob.at[head, rows_of(z)], out.at[:, columns(z, head)], out_recv).start()
        elif op == "o":
            give_back(head, *rest)

    sent = pl.ds(0, LOCAL_HEADS * (ULY - 1) * HDIM)
    for array in range(2):
        wait_bytes(kv_in[array].at[:, sent], send_sem.at[array])
    wait_bytes(q_in.at[:, sent], send_sem.at[2])
    for a, b in others:
        @if_inside(a, b)
        def _():
            index = (a + 1) * 3 + b + 1
            wait_bytes(kv.at[:, :, near(a), near(b)], halo_send.at[index])
            wait_bytes(cnt.at[4], cnt_send.at[index])
    wait_bytes(out.at[:, sent], out_send)
    wait_bytes(out, out_recv)


def on_device(queries, keys, values, window_mask, valid_count):
    heads = LOCAL_HEADS
    dma = pltpu.SemaphoreType.DMA
    return pl.pallas_call(
        kernel,
        out_shape=jax.ShapeDtypeStruct(queries.shape, queries.dtype),
        in_specs=[pl.BlockSpec(memory_space=pl.ANY)] * 5,
        out_specs=pl.BlockSpec(memory_space=pltpu.VMEM),
        scratch_shapes=[
            pltpu.VMEM((heads, 2, 4, 4, TILE, HDIM), jnp.bfloat16),
            pltpu.VMEM((heads, 256, HDIM), jnp.bfloat16),
            pltpu.VMEM((heads, 256, HDIM), jnp.bfloat16),
            pltpu.VMEM((9, 8, 128), jnp.int32),
            pltpu.VMEM((2, 2, 768), jnp.float32),
            pltpu.SMEM((4,), jnp.int32),
            pltpu.SMEM((4, 27), jnp.int32),
            dma((2,)), dma((3,)), dma((9,)), dma((9,)), dma,
            dma((heads, 2)), dma((heads,)), dma((heads, 2, 9)), dma((9,)), dma,
        ],
        compiler_params=pltpu.CompilerParams(
            collective_id=0, has_side_effects=True, vmem_limit_bytes=56 * 1024 * 1024),
    )(valid_count, window_mask, queries, keys, values)


def solution(mesh):
    in_specs = (
        P(("blk", "uly"), None),
        P(("blk", "uly"), None),
        P(("blk", "uly"), None),
        P("blk", None),
        P("blk"),
    )
    out_specs = P(("blk", "uly"), None)
    return jax.shard_map(
        on_device, mesh=mesh, in_specs=in_specs, out_specs=out_specs, check_vma=False
    )
```

```python
import math

import jax
import jax.numpy as jnp
from jax import lax
from jax.experimental import pallas as pl
from jax.experimental.pallas import tpu as pltpu
from jax.sharding import PartitionSpec as P

HDIM = 128
TILE = 64
ROWB, COLB = 4, 8
ULY = 16
HALF = ULY // 2
PART = 16
LOCAL_HEADS = 3
NEG = -1e30
EXP_SCALE = math.log2(math.e) / math.sqrt(HDIM)
MOVES = [(a, b) for a in (-1, 0, 1) for b in (-1, 0, 1)]
MESH = pl.DeviceIdType.MESH

ALL, FAR, NEAR = (0, ULY - 1), (0, 7), (7, ULY - 1)
def near(move):
    return pl.ds(1, 2) if move == 0 else pl.ds(2, 1) if move == 1 else pl.ds(1, 1)


def far(move):
    return pl.ds(1, 2) if move == 0 else pl.ds(0, 1) if move == 1 else pl.ds(3, 1)


def wait_bytes(ref, sem):
    pltpu.make_async_copy(ref, ref, sem).wait()


def kernel(count_in, mask_in, q_in, k_in, v_in, out, kv, qb, ob, cnt, bias, count_s, mask_s,
           small, send_sem, halo_send, cnt_send, out_send,
           in_recv, halo_recv, cnt_recv, out_recv):
    blk = lax.axis_index("blk")
    z = lax.axis_index("uly")
    half = z // HALF
    row, col = blk // COLB, blk % COLB

    up, down = row > 0, row < ROWB - 1
    left, right = col > 0, col < COLB - 1
    others = sorted((m for m in MOVES if m != (0, 0)), key=lambda m: -abs(m[0]) - abs(m[1]))
    barrier = pltpu.get_barrier_semaphore()
    cnt[...] = jnp.zeros_like(cnt)

    def to_neighbour(a, b):
        return (blk + a * COLB + b, z)

    def if_inside(a, b):
        inside = [have for have, wanted in ((up, a < 0), (down, a > 0), (left, b < 0), (right, b > 0)) if wanted]
        return pl.when(inside[0] if len(inside) == 1 else inside[0] & inside[1])

    def ring(step):
        return 8 + (step + 1) // 2 * (2 * lax.rem(step, 2) - 1)

    def greet(d, carry):
        pl.semaphore_signal(barrier, inc=1, device_id=(blk, lax.rem(z + ring(d), ULY)), device_id_type=MESH)
        return carry

    lax.fori_loop(0, ULY - 1, greet, 0)
    for a, b in others:
        @if_inside(a, b)
        def _():
            pl.semaphore_signal(barrier, inc=1, device_id=to_neighbour(a, b), device_id_type=MESH)

    def columns(peer, head):
        return pl.ds(pl.multiple_of((peer * LOCAL_HEADS + head) * HDIM, HDIM), HDIM)

    def rows_of(part):
        return pl.ds(pl.multiple_of(part * PART, PART), PART)

    def slot(array, head, part):
        if array == 2:
            return qb.at[head, rows_of(part)]
        return kv.at[head, array, 1 + part // HALF, 1 + lax.rem(part // 4, 2), rows_of(lax.rem(part, 4))]

    sources = (k_in, v_in, q_in)

    loads = [pltpu.make_async_copy(count_in, count_s, small.at[0]),
             pltpu.make_async_copy(mask_in, mask_s, small.at[1])]
    for copy in loads:
        copy.start()
    for head in range(LOCAL_HEADS):
        for array in range(3):
            pltpu.make_async_copy(sources[array].at[:, columns(z, head)], slot(array, head, z),
                                  in_recv.at[head, array]).start()

    for edge, at in ((~up, 0), (~down, 3)):
        @pl.when(edge)
        def _():
            kv[:, :, at:at + 1] = jnp.zeros((LOCAL_HEADS, 2, 1, 4, TILE, HDIM), kv.dtype)
    for edge, at in ((~left, 0), (~right, 3)):
        @pl.when(edge)
        def _():
            kv[:, :, :, at:at + 1] = jnp.zeros((LOCAL_HEADS, 2, 4, 1, TILE, HDIM), kv.dtype)

    across = 1 + left.astype(jnp.int32) + right.astype(jnp.int32)
    along = 1 + up.astype(jnp.int32) + down.astype(jnp.int32)
    pl.semaphore_wait(barrier, ULY - 2 + across * along)

    def scatter(array, head, steps):
        def body(step, carry):
            peer = lax.rem(z + ring(step), ULY)
            pltpu.make_async_remote_copy(
                src_ref=sources[array].at[:, columns(peer, head)],
                dst_ref=slot(array, head, z),
                send_sem=send_sem.at[array],
                recv_sem=in_recv.at[head, array],
                device_id=(blk, peer),
                device_id_type=MESH,
            ).start()
            return carry

        lax.fori_loop(*steps, body, 0)

    def send_counts():
        for copy in loads:
            copy.wait()
        for tile in range(8):
            cnt[4, tile:tile + 1, :] = jnp.full((1, 128), count_s[tile % 4], jnp.int32)
        for a, b in others:
            @if_inside(a, b)
            def _():
                index = (a + 1) * 3 + b + 1
                pltpu.make_async_remote_copy(
                    src_ref=cnt.at[4],
                    dst_ref=cnt.at[8 - index],
                    send_sem=cnt_send.at[index],
                    recv_sem=cnt_recv.at[index],
                    device_id=to_neighbour(a, b),
                    device_id_type=MESH,
                ).start()

    def halo(array, head):
        wait_bytes(qb.at[head], in_recv.at[head, array])
        for a, b in others:
            @if_inside(a, b)
            def _():
                index = (a + 1) * 3 + b + 1
                pltpu.make_async_remote_copy(
                    src_ref=kv.at[head, array, near(a), near(b)],
                    dst_ref=kv.at[head, array, far(a), far(b)],
                    send_sem=halo_send.at[index],
                    recv_sem=halo_recv.at[head, array, index],
                    device_id=to_neighbour(a, b),
                    device_id_type=MESH,
                ).start()

    def halo_arrived(array, head):
        for a, b in others:
            @if_inside(a, b)
            def _():
                wait_bytes(kv.at[head, array, far(-a), far(-b)],
                           halo_recv.at[head, array, (1 - a) * 3 + 1 - b])

    def build_bias():
        for a, b in others:
            @if_inside(a, b)
            def _():
                wait_bytes(cnt.at[0], cnt_recv.at[(1 - a) * 3 + 1 - b])
        lane = lax.broadcasted_iota(jnp.int32, (1, 128), 1)
        low = lane < TILE
        place = lax.rem(lane, TILE)

        def tile_count(r, c):
            a, b = (r + 1) // 2 - 1, (c + 1) // 2 - 1
            tile = (r + 1) % 2 * 2 + (c + 1) % 2
            return cnt[(a + 1) * 3 + b + 1, tile:tile + 1, :]

        for r in range(4):
            for pair in range(2):
                live = place < jnp.where(low, tile_count(r, 2 * pair), tile_count(r, 2 * pair + 1))
                for tile in range(4):
                    qr, qc = tile // 2, tile % 2
                    kr = r - qr
                    if not 0 <= kr < 3:
                        continue
                    picks = []
                    for c in (2 * pair, 2 * pair + 1):
                        e = c - qc
                        picks.append(mask_s[tile, 9 + 3 * kr + e] if 0 <= e < 3 else 0)
                    picked = jnp.where(low, picks[0], picks[1])
                    start = kr * 256 + pair * 128
                    bias[qr, qc:qc + 1, start:start + 128] = jnp.where(
                        live & (picked > 0), 0.0, NEG).astype(jnp.float32)

    def compute(head, qr):
        rows = pl.ds(pl.multiple_of(qr * 128, 128), 128)
        k = kv[head, 0, pl.ds(qr, 3)].reshape(768, HDIM)
        v = kv[head, 1, pl.ds(qr, 3)].reshape(768, HDIM)
        raw = lax.dot_general(qb[head, rows, :], k, (((1,), (1,)), ((), ())),
                              preferred_element_type=jnp.float32)
        raw = (raw.reshape(2, TILE, 768) + bias[qr].reshape(2, 1, 768)).reshape(128, 768)
        peak = jnp.max(raw, axis=1, keepdims=True)
        expo = jnp.exp2((raw - peak) * EXP_SCALE)
        total = jnp.sum(expo, axis=1, keepdims=True)
        summed = jnp.dot(expo.astype(jnp.bfloat16), v, preferred_element_type=jnp.float32)
        ob[head, rows, :] = (summed / total).astype(jnp.bfloat16)

    def give_back(head, part_row):
        def body(step, carry):
            peer = part_row * HALF + step

            @pl.when(peer != z)
            def _():
                pltpu.make_async_remote_copy(
                    src_ref=ob.at[head, rows_of(peer)],
                    dst_ref=out.at[:, columns(z, head)],
                    send_sem=out_send,
                    recv_sem=out_recv,
                    device_id=(blk, peer),
                    device_id_type=MESH,
                ).start()

            return carry

        lax.fori_loop(0, HALF, body, 0)

    scatter(0, 0, ALL)
    scatter(1, 0, ALL)
    send_counts()
    scatter(0, 1, ALL)
    scatter(1, 1, ALL)
    scatter(2, 0, ALL)
    scatter(0, 2, ALL)
    scatter(1, 2, ALL)
    for steps in (FAR, NEAR):
        for head in (1, 2):
            scatter(2, head, steps)

    def turn(i, carry):
        @pl.when(i < LOCAL_HEADS)
        def _():
            lax.fori_loop(0, 2, lambda array, carry: halo(array, i), None)

        @pl.when(i == 0)
        def _():
            build_bias()

        @pl.when(i > 0)
        def _():
            head = i - 1
            lax.fori_loop(0, 2, lambda array, carry: halo_arrived(array, head), None)
            wait_bytes(qb.at[head], in_recv.at[head, 2])
            compute(head, 0)
            give_back(head, 0)
            compute(head, 1)
            pltpu.make_async_copy(ob.at[head, rows_of(z)], out.at[:, columns(z, head)], out_recv).start()

            @pl.when(head == 0)
            def _():
                give_back(head, 1)

        return carry

    lax.fori_loop(0, LOCAL_HEADS + 1, turn, 0)
    give_back(1, 1)
    give_back(2, 1)

    sent = pl.ds(0, LOCAL_HEADS * (ULY - 1) * HDIM)
    for array in range(3):
        wait_bytes(sources[array].at[:, sent], send_sem.at[array])
    for a, b in others:
        @if_inside(a, b)
        def _():
            index = (a + 1) * 3 + b + 1
            wait_bytes(kv.at[:, :, near(a), near(b)], halo_send.at[index])
            wait_bytes(cnt.at[4], cnt_send.at[index])
    wait_bytes(out.at[:, sent], out_send)
    wait_bytes(out, out_recv)


def on_device(queries, keys, values, window_mask, valid_count):
    heads = LOCAL_HEADS
    dma = pltpu.SemaphoreType.DMA
    return pl.pallas_call(
        kernel,
        out_shape=jax.ShapeDtypeStruct(queries.shape, queries.dtype),
        in_specs=[pl.BlockSpec(memory_space=pl.ANY)] * 5,
        out_specs=pl.BlockSpec(memory_space=pltpu.VMEM),
        scratch_shapes=[
            pltpu.VMEM((heads, 2, 4, 4, TILE, HDIM), jnp.bfloat16),
            pltpu.VMEM((heads, 256, HDIM), jnp.bfloat16),
            pltpu.VMEM((heads, 256, HDIM), jnp.bfloat16),
            pltpu.VMEM((9, 8, 128), jnp.int32),
            pltpu.VMEM((2, 2, 768), jnp.float32),
            pltpu.SMEM((4,), jnp.int32),
            pltpu.SMEM((4, 27), jnp.int32),
            dma((2,)), dma((3,)), dma((9,)), dma((9,)), dma,
            dma((heads, 3)), dma((heads, 2, 9)), dma((9,)), dma,
        ],
        compiler_params=pltpu.CompilerParams(
            collective_id=0, has_side_effects=True, vmem_limit_bytes=56 * 1024 * 1024),
    )(valid_count, window_mask, queries, keys, values)


def solution(mesh):
    in_specs = (
        P(("blk", "uly"), None),
        P(("blk", "uly"), None),
        P(("blk", "uly"), None),
        P("blk", None),
        P("blk"),
    )
    out_specs = P(("blk", "uly"), None)
    return jax.shard_map(
        on_device, mesh=mesh, in_specs=in_specs, out_specs=out_specs, check_vma=False
    )
```

```python
import math

import jax
import jax.numpy as jnp
from jax import lax
from jax.experimental import pallas as pl
from jax.experimental.pallas import tpu as pltpu
from jax.sharding import PartitionSpec as P

HDIM = 128
TILE = 64
ROWB, COLB = 4, 8
ULY = 16
HALF = ULY // 2
PART = 16
LOCAL_HEADS = 3
NEG = -1e30
EXP_SCALE = math.log2(math.e) / math.sqrt(HDIM)
MOVES = [(a, b) for a in (-1, 0, 1) for b in (-1, 0, 1)]
MESH = pl.DeviceIdType.MESH

ALL, FAR, NEAR = (0, ULY - 1), (0, 7), (7, ULY - 1)


def near(move):
    return pl.ds(1, 2) if move == 0 else pl.ds(2, 1) if move == 1 else pl.ds(1, 1)


def far(move):
    return pl.ds(1, 2) if move == 0 else pl.ds(0, 1) if move == 1 else pl.ds(3, 1)


def wait_bytes(ref, sem):
    pltpu.make_async_copy(ref, ref, sem).wait()


def kernel(count_in, mask_in, q_in, k_in, v_in, out, kv, qb, ob, cnt, bias, count_s, mask_s,
           small, send_sem, halo_send, cnt_send, out_send,
           in_recv, halo_recv, cnt_recv, out_recv):
    blk = lax.axis_index("blk")
    z = lax.axis_index("uly")
    half = z // HALF
    core = lax.rem(blk, 2)
    row, col = blk // COLB, blk % COLB

    up, down = row > 0, row < ROWB - 1
    left, right = col > 0, col < COLB - 1
    others = sorted((m for m in MOVES if m != (0, 0)), key=lambda m: -abs(m[0]) - abs(m[1]))
    barrier = pltpu.get_barrier_semaphore()
    cnt[...] = jnp.zeros_like(cnt)

    def to_neighbour(a, b):
        return (blk + a * COLB + b, z)

    def if_inside(a, b):
        inside = [have for have, wanted in ((up, a < 0), (down, a > 0), (left, b < 0), (right, b > 0)) if wanted]
        return pl.when(inside[0] if len(inside) == 1 else inside[0] & inside[1])

    def ring(step):
        return 8 + (step + 1) // 2 * (2 * lax.rem(step, 2) - 1)

    def greet(d, carry):
        pl.semaphore_signal(barrier, inc=1, device_id=(blk, lax.rem(z + ring(d), ULY)), device_id_type=MESH)
        return carry

    lax.fori_loop(0, ULY - 1, greet, 0)
    for a, b in others:
        @if_inside(a, b)
        def _():
            pl.semaphore_signal(barrier, inc=1, device_id=to_neighbour(a, b), device_id_type=MESH)

    def columns(peer, head):
        return pl.ds(pl.multiple_of((peer * LOCAL_HEADS + head) * HDIM, HDIM), HDIM)

    def rows_of(part):
        return pl.ds(pl.multiple_of(part * PART, PART), PART)

    def slot(array, head, part):
        if array == 2:
            return qb.at[head, rows_of(part)]
        return kv.at[head, array, 1 + part // HALF, 1 + lax.rem(part // 4, 2), rows_of(lax.rem(part, 4))]

    sources = (k_in, v_in, q_in)

    loads = [pltpu.make_async_copy(count_in, count_s, small.at[0]),
             pltpu.make_async_copy(mask_in, mask_s, small.at[1])]
    for copy in loads:
        copy.start()
    for head in range(LOCAL_HEADS):
        for array in range(3):
            pltpu.make_async_copy(sources[array].at[:, columns(z, head)], slot(array, head, z),
                                  in_recv.at[head, array]).start()

    for edge, at in ((~up, 0), (~down, 3)):
        @pl.when(edge)
        def _():
            kv[:, :, at:at + 1] = jnp.zeros((LOCAL_HEADS, 2, 1, 4, TILE, HDIM), kv.dtype)
    for edge, at in ((~left, 0), (~right, 3)):
        @pl.when(edge)
        def _():
            kv[:, :, :, at:at + 1] = jnp.zeros((LOCAL_HEADS, 2, 4, 1, TILE, HDIM), kv.dtype)

    across = 1 + left.astype(jnp.int32) + right.astype(jnp.int32)
    along = 1 + up.astype(jnp.int32) + down.astype(jnp.int32)
    pl.semaphore_wait(barrier, ULY - 2 + across * along)

    def scatter(array, head, steps):
        def body(step, carry):
            peer = lax.rem(z + ring(step), ULY)
            pltpu.make_async_remote_copy(
                src_ref=sources[array].at[:, columns(peer, head)],
                dst_ref=slot(array, head, z),
                send_sem=send_sem.at[array],
                recv_sem=in_recv.at[head, array],
                device_id=(blk, peer),
                device_id_type=MESH,
            ).start()
            return carry

        lax.fori_loop(*steps, body, 0)

    def send_counts():
        for copy in loads:
            copy.wait()
        for tile in range(8):
            cnt[4, tile:tile + 1, :] = jnp.full((1, 128), count_s[tile % 4], jnp.int32)
        for a, b in others:
            @if_inside(a, b)
            def _():
                index = (a + 1) * 3 + b + 1
                pltpu.make_async_remote_copy(
                    src_ref=cnt.at[4],
                    dst_ref=cnt.at[8 - index],
                    send_sem=cnt_send.at[index],
                    recv_sem=cnt_recv.at[index],
                    device_id=to_neighbour(a, b),
                    device_id_type=MESH,
                ).start()

    def halo(array, head):
        wait_bytes(qb.at[head], in_recv.at[head, array])
        for a, b in others:
            @if_inside(a, b)
            def _():
                index = (a + 1) * 3 + b + 1
                pltpu.make_async_remote_copy(
                    src_ref=kv.at[head, array, near(a), near(b)],
                    dst_ref=kv.at[head, array, far(a), far(b)],
                    send_sem=halo_send.at[index],
                    recv_sem=halo_recv.at[head, array, index],
                    device_id=to_neighbour(a, b),
                    device_id_type=MESH,
                ).start()

    def halo_arrived(array, head):
        for a, b in others:
            @if_inside(a, b)
            def _():
                wait_bytes(kv.at[head, array, far(-a), far(-b)],
                           halo_recv.at[head, array, (1 - a) * 3 + 1 - b])

    def build_bias():
        for a, b in others:
            @if_inside(a, b)
            def _():
                wait_bytes(cnt.at[0], cnt_recv.at[(1 - a) * 3 + 1 - b])
        lane = lax.broadcasted_iota(jnp.int32, (1, 128), 1)
        low = lane < TILE
        place = lax.rem(lane, TILE)

        def tile_count(r, c):
            a, b = (r + 1) // 2 - 1, (c + 1) // 2 - 1
            tile = (r + 1) % 2 * 2 + (c + 1) % 2
            return cnt[(a + 1) * 3 + b + 1, tile:tile + 1, :]

        for r in range(4):
            for pair in range(2):
                live = place < jnp.where(low, tile_count(r, 2 * pair), tile_count(r, 2 * pair + 1))
                for tile in range(4):
                    qr, qc = tile // 2, tile % 2
                    kr = r - qr
                    if not 0 <= kr < 3:
                        continue
                    picks = []
                    for c in (2 * pair, 2 * pair + 1):
                        e = c - qc
                        picks.append(mask_s[tile, 9 + 3 * kr + e] if 0 <= e < 3 else 0)
                    picked = jnp.where(low, picks[0], picks[1])
                    start = kr * 256 + pair * 128
                    bias[qr, qc:qc + 1, start:start + 128] = jnp.where(
                        live & (picked > 0), 0.0, NEG).astype(jnp.float32)

    def compute(head, qr):
        rows = pl.ds(pl.multiple_of(qr * 128, 128), 128)
        k = kv[head, 0, pl.ds(qr, 3)].reshape(768, HDIM)
        v = kv[head, 1, pl.ds(qr, 3)].reshape(768, HDIM)
        raw = lax.dot_general(qb[head, rows, :], k, (((1,), (1,)), ((), ())),
                              preferred_element_type=jnp.float32)
        raw = (raw.reshape(2, TILE, 768) + bias[qr].reshape(2, 1, 768)).reshape(128, 768)
        peak = jnp.max(raw, axis=1, keepdims=True)
        expo = jnp.exp2((raw - peak) * EXP_SCALE)
        total = jnp.sum(expo, axis=1, keepdims=True)
        summed = jnp.dot(expo.astype(jnp.bfloat16), v, preferred_element_type=jnp.float32)
        ob[head, rows, :] = (summed / total).astype(jnp.bfloat16)

    def give_back(head, part_row):
        def body(step, carry):
            peer = part_row * HALF + step

            @pl.when(peer != z)
            def _():
                pltpu.make_async_remote_copy(
                    src_ref=ob.at[head, rows_of(peer)],
                    dst_ref=out.at[:, columns(z, head)],
                    send_sem=out_send,
                    recv_sem=out_recv,
                    device_id=(blk, peer),
                    device_id_type=MESH,
                ).start()

            return carry

        lax.fori_loop(0, HALF, body, 0)

    scatter(0, 0, ALL)
    scatter(1, 0, ALL)
    send_counts()
    scatter(0, 1, ALL)
    scatter(1, 1, ALL)
    scatter(2, 0, ALL)
    scatter(0, 2, ALL)
    scatter(1, 2, ALL)
    for steps in (FAR, NEAR):
        for head in (1, 2):
            scatter(2, head, steps)

    def turn(i, carry):
        @pl.when(i < LOCAL_HEADS)
        def _():
            lax.fori_loop(0, 2, lambda array, carry: halo(array, i), None)

        @pl.when(i == 0)
        def _():
            build_bias()

        @pl.when(i > 0)
        def _():
            head = i - 1
            lax.fori_loop(0, 2, lambda array, carry: halo_arrived(array, head), None)
            wait_bytes(qb.at[head], in_recv.at[head, 2])
            first = jnp.where(head == 1, core, 0)

            def attend(row):
                compute(head, row)
                give_back(head, row)

            attend(first)
            pl.when((head == 0) | ((head == 1) & (core == 1)))(lambda: attend(1 - first))

        return carry

    lax.fori_loop(0, LOCAL_HEADS + 1, turn, 0)

    @pl.when(core == 0)
    def _():
        compute(1, 1)
        give_back(1, 1)
        compute(2, 1)
        give_back(2, 1)

    @pl.when(core == 1)
    def _():
        compute(2, 1)
        give_back(2, 1)

    for head in range(LOCAL_HEADS):
        pltpu.make_async_copy(ob.at[head, rows_of(z)], out.at[:, columns(z, head)], out_recv).start()

    sent = pl.ds(0, LOCAL_HEADS * (ULY - 1) * HDIM)
    for array in range(3):
        wait_bytes(sources[array].at[:, sent], send_sem.at[array])
    for a, b in others:
        @if_inside(a, b)
        def _():
            index = (a + 1) * 3 + b + 1
            wait_bytes(kv.at[:, :, near(a), near(b)], halo_send.at[index])
            wait_bytes(cnt.at[4], cnt_send.at[index])
    wait_bytes(out.at[:, sent], out_send)
    wait_bytes(out, out_recv)


def on_device(queries, keys, values, window_mask, valid_count):
    heads = LOCAL_HEADS
    dma = pltpu.SemaphoreType.DMA
    return pl.pallas_call(
        kernel,
        out_shape=jax.ShapeDtypeStruct(queries.shape, queries.dtype),
        in_specs=[pl.BlockSpec(memory_space=pl.ANY)] * 5,
        out_specs=pl.BlockSpec(memory_space=pltpu.VMEM),
        scratch_shapes=[
            pltpu.VMEM((heads, 2, 4, 4, TILE, HDIM), jnp.bfloat16),
            pltpu.VMEM((heads, 256, HDIM), jnp.bfloat16),
            pltpu.VMEM((heads, 256, HDIM), jnp.bfloat16),
            pltpu.VMEM((9, 8, 128), jnp.int32),
            pltpu.VMEM((2, 2, 768), jnp.float32),
            pltpu.SMEM((4,), jnp.int32),
            pltpu.SMEM((4, 27), jnp.int32),
            dma((2,)), dma((3,)), dma((9,)), dma((9,)), dma,
            dma((heads, 3)), dma((heads, 2, 9)), dma((9,)), dma,
        ],
        compiler_params=pltpu.CompilerParams(
            collective_id=0, has_side_effects=True, vmem_limit_bytes=56 * 1024 * 1024),
    )(valid_count, window_mask, queries, keys, values)


def solution(mesh):
    in_specs = (
        P(("blk", "uly"), None),
        P(("blk", "uly"), None),
        P(("blk", "uly"), None),
        P("blk", None),
        P("blk"),
    )
    out_specs = P(("blk", "uly"), None)
    return jax.shard_map(
        on_device, mesh=mesh, in_specs=in_specs, out_specs=out_specs, check_vma=False
    )
```

```python
import math

import jax
import jax.numpy as jnp
from jax import lax
from jax.experimental import pallas as pl
from jax.experimental.pallas import tpu as pltpu
from jax.sharding import PartitionSpec as P

HDIM = 128
TILE = 64
ROWB, COLB = 4, 8
ULY = 16
HALF = ULY // 2
PART = 16
LOCAL_HEADS = 3
NEG = -1e30
EXP_SCALE = math.log2(math.e) / math.sqrt(HDIM)
MOVES = [(a, b) for a in (-1, 0, 1) for b in (-1, 0, 1)]
MESH = pl.DeviceIdType.MESH

ALL, FAR, NEAR = (0, ULY - 1), (0, 7), (7, ULY - 1)


def near(move):
    return pl.ds(1, 2) if move == 0 else pl.ds(2, 1) if move == 1 else pl.ds(1, 1)


def far(move):
    return pl.ds(1, 2) if move == 0 else pl.ds(0, 1) if move == 1 else pl.ds(3, 1)


def wait_bytes(ref, sem):
    pltpu.make_async_copy(ref, ref, sem).wait()


def kernel(count_in, mask_in, q_in, k_in, v_in, out, kv, qb, ob, cnt, bias, count_s, mask_s,
           small, send_sem, halo_send, cnt_send, out_send,
           in_recv, halo_recv, cnt_recv, out_recv, staged, stage_sem):
    blk = lax.axis_index("blk")
    z = lax.axis_index("uly")
    half = z // HALF
    core = lax.rem(blk, 2)
    row, col = blk // COLB, blk % COLB

    up, down = row > 0, row < ROWB - 1
    left, right = col > 0, col < COLB - 1
    others = sorted((m for m in MOVES if m != (0, 0)), key=lambda m: -abs(m[0]) - abs(m[1]))
    barrier = pltpu.get_barrier_semaphore()
    cnt[...] = jnp.zeros_like(cnt)

    def to_neighbour(a, b):
        return (blk + a * COLB + b, z)

    def if_inside(a, b):
        inside = [have for have, wanted in ((up, a < 0), (down, a > 0), (left, b < 0), (right, b > 0)) if wanted]
        return pl.when(inside[0] if len(inside) == 1 else inside[0] & inside[1])

    def ring(step):
        return 8 + (step + 1) // 2 * (2 * lax.rem(step, 2) - 1)

    def greet(d, carry):
        pl.semaphore_signal(barrier, inc=1, device_id=(blk, lax.rem(z + ring(d), ULY)), device_id_type=MESH)
        return carry

    lax.fori_loop(0, ULY - 1, greet, 0)
    for a, b in others:
        @if_inside(a, b)
        def _():
            pl.semaphore_signal(barrier, inc=1, device_id=to_neighbour(a, b), device_id_type=MESH)

    def columns(peer, head):
        return pl.ds(pl.multiple_of((peer * LOCAL_HEADS + head) * HDIM, HDIM), HDIM)

    def rows_of(part):
        return pl.ds(pl.multiple_of(part * PART, PART), PART)

    def slot(array, head, part):
        if array == 2:
            return qb.at[head, rows_of(part)]
        return kv.at[head, array, 1 + part // HALF, 1 + lax.rem(part // 4, 2), rows_of(lax.rem(part, 4))]

    stages = [pltpu.make_async_copy(source, staged.at[array], stage_sem.at[array])
              for array, source in enumerate((k_in, v_in, q_in))]
    for copy in stages:
        copy.start()
    sources = [staged.at[array] for array in range(3)]

    loads = [pltpu.make_async_copy(count_in, count_s, small.at[0]),
             pltpu.make_async_copy(mask_in, mask_s, small.at[1])]
    for copy in loads:
        copy.start()
    for head in range(LOCAL_HEADS):
        for array in range(3):
            pltpu.make_async_copy((k_in, v_in, q_in)[array].at[:, columns(z, head)], slot(array, head, z),
                                  in_recv.at[head, array]).start()

    for edge, at in ((~up, 0), (~down, 3)):
        @pl.when(edge)
        def _():
            kv[:, :, at:at + 1] = jnp.zeros((LOCAL_HEADS, 2, 1, 4, TILE, HDIM), kv.dtype)
    for edge, at in ((~left, 0), (~right, 3)):
        @pl.when(edge)
        def _():
            kv[:, :, :, at:at + 1] = jnp.zeros((LOCAL_HEADS, 2, 4, 1, TILE, HDIM), kv.dtype)

    across = 1 + left.astype(jnp.int32) + right.astype(jnp.int32)
    along = 1 + up.astype(jnp.int32) + down.astype(jnp.int32)
    for copy in stages:
        copy.wait()
    pl.semaphore_wait(barrier, ULY - 2 + across * along)

    def scatter(array, head, steps):
        def body(step, carry):
            peer = lax.rem(z + ring(step), ULY)
            pltpu.make_async_remote_copy(
                src_ref=sources[array].at[:, columns(peer, head)],
                dst_ref=slot(array, head, z),
                send_sem=send_sem.at[array],
                recv_sem=in_recv.at[head, array],
                device_id=(blk, peer),
                device_id_type=MESH,
            ).start()
            return carry

        lax.fori_loop(*steps, body, 0)

    def send_counts():
        for copy in loads:
            copy.wait()
        for tile in range(8):
            cnt[4, tile:tile + 1, :] = jnp.full((1, 128), count_s[tile % 4], jnp.int32)
        for a, b in others:
            @if_inside(a, b)
            def _():
                index = (a + 1) * 3 + b + 1
                pltpu.make_async_remote_copy(
                    src_ref=cnt.at[4],
                    dst_ref=cnt.at[8 - index],
                    send_sem=cnt_send.at[index],
                    recv_sem=cnt_recv.at[index],
                    device_id=to_neighbour(a, b),
                    device_id_type=MESH,
                ).start()

    def halo(array, head):
        wait_bytes(qb.at[head], in_recv.at[head, array])
        for a, b in others:
            @if_inside(a, b)
            def _():
                index = (a + 1) * 3 + b + 1
                pltpu.make_async_remote_copy(
                    src_ref=kv.at[head, array, near(a), near(b)],
                    dst_ref=kv.at[head, array, far(a), far(b)],
                    send_sem=halo_send.at[index],
                    recv_sem=halo_recv.at[head, array, index],
                    device_id=to_neighbour(a, b),
                    device_id_type=MESH,
                ).start()

    def halo_arrived(array, head):
        for a, b in others:
            @if_inside(a, b)
            def _():
                wait_bytes(kv.at[head, array, far(-a), far(-b)],
                           halo_recv.at[head, array, (1 - a) * 3 + 1 - b])

    def build_bias():
        for a, b in others:
            @if_inside(a, b)
            def _():
                wait_bytes(cnt.at[0], cnt_recv.at[(1 - a) * 3 + 1 - b])
        lane = lax.broadcasted_iota(jnp.int32, (1, 128), 1)
        low = lane < TILE
        place = lax.rem(lane, TILE)

        def tile_count(r, c):
            a, b = (r + 1) // 2 - 1, (c + 1) // 2 - 1
            tile = (r + 1) % 2 * 2 + (c + 1) % 2
            return cnt[(a + 1) * 3 + b + 1, tile:tile + 1, :]

        for r in range(4):
            for pair in range(2):
                live = place < jnp.where(low, tile_count(r, 2 * pair), tile_count(r, 2 * pair + 1))
                for tile in range(4):
                    qr, qc = tile // 2, tile % 2
                    kr = r - qr
                    if not 0 <= kr < 3:
                        continue
                    picks = []
                    for c in (2 * pair, 2 * pair + 1):
                        e = c - qc
                        picks.append(mask_s[tile, 9 + 3 * kr + e] if 0 <= e < 3 else 0)
                    picked = jnp.where(low, picks[0], picks[1])
                    start = kr * 256 + pair * 128
                    bias[qr, qc:qc + 1, start:start + 128] = jnp.where(
                        live & (picked > 0), 0.0, NEG).astype(jnp.float32)

    def compute(head, qr):
        rows = pl.ds(pl.multiple_of(qr * 128, 128), 128)
        k = kv[head, 0, pl.ds(qr, 3)].reshape(768, HDIM)
        v = kv[head, 1, pl.ds(qr, 3)].reshape(768, HDIM)
        raw = lax.dot_general(qb[head, rows, :], k, (((1,), (1,)), ((), ())),
                              preferred_element_type=jnp.float32)
        raw = (raw.reshape(2, TILE, 768) + bias[qr].reshape(2, 1, 768)).reshape(128, 768)
        peak = jnp.max(raw, axis=1, keepdims=True)
        expo = jnp.exp2((raw - peak) * EXP_SCALE)
        total = jnp.sum(expo, axis=1, keepdims=True)
        summed = jnp.dot(expo.astype(jnp.bfloat16), v, preferred_element_type=jnp.float32)
        ob[head, rows, :] = (summed / total).astype(jnp.bfloat16)

    def give_back(head, part_row):
        def body(step, carry):
            peer = part_row * HALF + step

            @pl.when(peer != z)
            def _():
                pltpu.make_async_remote_copy(
                    src_ref=ob.at[head, rows_of(peer)],
                    dst_ref=out.at[:, columns(z, head)],
                    send_sem=out_send,
                    recv_sem=out_recv,
                    device_id=(blk, peer),
                    device_id_type=MESH,
                ).start()

            return carry

        lax.fori_loop(0, HALF, body, 0)

    scatter(0, 0, ALL)
    scatter(1, 0, ALL)
    send_counts()
    scatter(0, 1, ALL)
    scatter(1, 1, ALL)
    scatter(2, 0, ALL)
    scatter(0, 2, ALL)
    scatter(1, 2, ALL)
    for steps in (FAR, NEAR):
        for head in (1, 2):
            scatter(2, head, steps)

    def turn(i, carry):
        @pl.when(i < LOCAL_HEADS)
        def _():
            lax.fori_loop(0, 2, lambda array, carry: halo(array, i), None)

        @pl.when(i == 0)
        def _():
            build_bias()

        @pl.when(i > 0)
        def _():
            head = i - 1
            lax.fori_loop(0, 2, lambda array, carry: halo_arrived(array, head), None)
            wait_bytes(qb.at[head], in_recv.at[head, 2])
            first = jnp.where(head == 1, core, 0)

            def attend(row):
                compute(head, row)
                give_back(head, row)

            attend(first)
            pl.when((head == 0) | ((head == 1) & (core == 1)))(lambda: attend(1 - first))

        return carry

    lax.fori_loop(0, LOCAL_HEADS + 1, turn, 0)

    @pl.when(core == 0)
    def _():
        compute(1, 1)
        give_back(1, 1)
        compute(2, 1)
        give_back(2, 1)

    @pl.when(core == 1)
    def _():
        compute(2, 1)
        give_back(2, 1)

    for head in range(LOCAL_HEADS):
        pltpu.make_async_copy(ob.at[head, rows_of(z)], out.at[:, columns(z, head)], out_recv).start()

    sent = pl.ds(0, LOCAL_HEADS * (ULY - 1) * HDIM)
    for array in range(3):
        wait_bytes(sources[array].at[:, sent], send_sem.at[array])
    for a, b in others:
        @if_inside(a, b)
        def _():
            index = (a + 1) * 3 + b + 1
            wait_bytes(kv.at[:, :, near(a), near(b)], halo_send.at[index])
            wait_bytes(cnt.at[4], cnt_send.at[index])
    wait_bytes(out.at[:, sent], out_send)
    wait_bytes(out, out_recv)


def on_device(queries, keys, values, window_mask, valid_count):
    heads = LOCAL_HEADS
    dma = pltpu.SemaphoreType.DMA
    return pl.pallas_call(
        kernel,
        out_shape=jax.ShapeDtypeStruct(queries.shape, queries.dtype),
        in_specs=[pl.BlockSpec(memory_space=pl.ANY)] * 5,
        out_specs=pl.BlockSpec(memory_space=pltpu.VMEM),
        scratch_shapes=[
            pltpu.VMEM((heads, 2, 4, 4, TILE, HDIM), jnp.bfloat16),
            pltpu.VMEM((heads, 256, HDIM), jnp.bfloat16),
            pltpu.VMEM((heads, 256, HDIM), jnp.bfloat16),
            pltpu.VMEM((9, 8, 128), jnp.int32),
            pltpu.VMEM((2, 2, 768), jnp.float32),
            pltpu.SMEM((4,), jnp.int32),
            pltpu.SMEM((4, 27), jnp.int32),
            dma((2,)), dma((3,)), dma((9,)), dma((9,)), dma,
            dma((heads, 3)), dma((heads, 2, 9)), dma((9,)), dma,
            pltpu.VMEM((3,) + queries.shape, jnp.bfloat16), dma((3,)),
        ],
        compiler_params=pltpu.CompilerParams(
            collective_id=0, has_side_effects=True, vmem_limit_bytes=56 * 1024 * 1024),
    )(valid_count, window_mask, queries, keys, values)


def solution(mesh):
    in_specs = (
        P(("blk", "uly"), None),
        P(("blk", "uly"), None),
        P(("blk", "uly"), None),
        P("blk", None),
        P("blk"),
    )
    out_specs = P(("blk", "uly"), None)
    return jax.shard_map(
        on_device, mesh=mesh, in_specs=in_specs, out_specs=out_specs, check_vma=False
    )
```

```python
import math

import jax
import jax.numpy as jnp
from jax import lax
from jax.experimental import pallas as pl
from jax.experimental.pallas import tpu as pltpu
from jax.sharding import PartitionSpec as P

HDIM = 128
TILE = 64
ROWB, COLB = 4, 8
ULY = 16
HALF = ULY // 2
PART = 16
LOCAL_HEADS = 3
NEG = -1e30
EXP_SCALE = math.log2(math.e) / math.sqrt(HDIM)
MOVES = [(a, b) for a in (-1, 0, 1) for b in (-1, 0, 1)]
MESH = pl.DeviceIdType.MESH

ALL, FAR, NEAR = (0, ULY - 1), (0, 7), (7, ULY - 1)


def near(move):
    return pl.ds(1, 2) if move == 0 else pl.ds(2, 1) if move == 1 else pl.ds(1, 1)


def far(move):
    return pl.ds(1, 2) if move == 0 else pl.ds(0, 1) if move == 1 else pl.ds(3, 1)


def wait_bytes(ref, sem):
    pltpu.make_async_copy(ref, ref, sem).wait()


def kernel(count_in, mask_in, q_in, k_in, v_in, out, kv, qb, ob, cnt, bias, count_s, mask_s,
           small, send_sem, halo_send, cnt_send, out_send,
           in_recv, halo_recv, cnt_recv, out_recv, staged, stage_sem):
    blk = lax.axis_index("blk")
    z = lax.axis_index("uly")
    half = z // HALF
    core = lax.rem(blk, 2)
    row, col = blk // COLB, blk % COLB

    up, down = row > 0, row < ROWB - 1
    left, right = col > 0, col < COLB - 1
    others = sorted((m for m in MOVES if m != (0, 0)), key=lambda m: -abs(m[0]) - abs(m[1]))
    barrier = pltpu.get_barrier_semaphore()
    cnt[...] = jnp.zeros_like(cnt)

    def to_neighbour(a, b):
        return (blk + a * COLB + b, z)

    def if_inside(a, b):
        inside = [have for have, wanted in ((up, a < 0), (down, a > 0), (left, b < 0), (right, b > 0)) if wanted]
        return pl.when(inside[0] if len(inside) == 1 else inside[0] & inside[1])

    def ring(step):
        return 8 + (step + 1) // 2 * (2 * lax.rem(step, 2) - 1)

    def greet(d, carry):
        pl.semaphore_signal(barrier, inc=1, device_id=(blk, lax.rem(z + ring(d), ULY)), device_id_type=MESH)
        return carry

    lax.fori_loop(0, ULY - 1, greet, 0)
    for a, b in others:
        @if_inside(a, b)
        def _():
            pl.semaphore_signal(barrier, inc=1, device_id=to_neighbour(a, b), device_id_type=MESH)

    def columns(peer, head):
        return pl.ds(pl.multiple_of((peer * LOCAL_HEADS + head) * HDIM, HDIM), HDIM)

    def rows_of(part):
        return pl.ds(pl.multiple_of(part * PART, PART), PART)

    def slot(array, head, part):
        if array == 2:
            return qb.at[head, rows_of(part)]
        return kv.at[head, array, 1 + part // HALF, 1 + lax.rem(part // 4, 2), rows_of(lax.rem(part, 4))]

    stages = [pltpu.make_async_copy(source, staged.at[array], stage_sem.at[array])
              for array, source in enumerate((k_in, v_in, q_in))]
    for copy in stages:
        copy.start()
    sources = [staged.at[array] for array in range(3)]

    loads = [pltpu.make_async_copy(count_in, count_s, small.at[0]),
             pltpu.make_async_copy(mask_in, mask_s, small.at[1])]
    for copy in loads:
        copy.start()
    for head in range(LOCAL_HEADS):
        for array in range(3):
            pltpu.make_async_copy((k_in, v_in, q_in)[array].at[:, columns(z, head)], slot(array, head, z),
                                  in_recv.at[head, array]).start()

    for edge, at in ((~up, 0), (~down, 3)):
        @pl.when(edge)
        def _():
            kv[:, :, at:at + 1] = jnp.zeros((LOCAL_HEADS, 2, 1, 4, TILE, HDIM), kv.dtype)
    for edge, at in ((~left, 0), (~right, 3)):
        @pl.when(edge)
        def _():
            kv[:, :, :, at:at + 1] = jnp.zeros((LOCAL_HEADS, 2, 4, 1, TILE, HDIM), kv.dtype)

    across = 1 + left.astype(jnp.int32) + right.astype(jnp.int32)
    along = 1 + up.astype(jnp.int32) + down.astype(jnp.int32)
    for copy in stages:
        copy.wait()
    pl.semaphore_wait(barrier, ULY - 2 + across * along)

    def scatter(array, head, steps):
        def body(step, carry):
            peer = lax.rem(z + ring(step), ULY)
            pltpu.make_async_remote_copy(
                src_ref=sources[array].at[:, columns(peer, head)],
                dst_ref=slot(array, head, z),
                send_sem=send_sem.at[array],
                recv_sem=in_recv.at[head, array],
                device_id=(blk, peer),
                device_id_type=MESH,
            ).start()
            return carry

        lax.fori_loop(*steps, body, 0)

    def send_counts():
        for copy in loads:
            copy.wait()
        for tile in range(8):
            cnt[4, tile:tile + 1, :] = jnp.full((1, 128), count_s[tile % 4], jnp.int32)
        for a, b in others:
            @if_inside(a, b)
            def _():
                index = (a + 1) * 3 + b + 1
                pltpu.make_async_remote_copy(
                    src_ref=cnt.at[4],
                    dst_ref=cnt.at[8 - index],
                    send_sem=cnt_send.at[index],
                    recv_sem=cnt_recv.at[index],
                    device_id=to_neighbour(a, b),
                    device_id_type=MESH,
                ).start()

    def halo(array, head):
        wait_bytes(qb.at[head], in_recv.at[head, array])
        for a, b in others:
            @if_inside(a, b)
            def _():
                index = (a + 1) * 3 + b + 1
                pltpu.make_async_remote_copy(
                    src_ref=kv.at[head, array, near(a), near(b)],
                    dst_ref=kv.at[head, array, far(a), far(b)],
                    send_sem=halo_send.at[index],
                    recv_sem=halo_recv.at[head, array, index],
                    device_id=to_neighbour(a, b),
                    device_id_type=MESH,
                ).start()

    def halo_arrived(array, head):
        for a, b in others:
            @if_inside(a, b)
            def _():
                wait_bytes(kv.at[head, array, far(-a), far(-b)],
                           halo_recv.at[head, array, (1 - a) * 3 + 1 - b])

    def build_bias():
        for a, b in others:
            @if_inside(a, b)
            def _():
                wait_bytes(cnt.at[0], cnt_recv.at[(1 - a) * 3 + 1 - b])
        lane = lax.broadcasted_iota(jnp.int32, (1, 128), 1)
        low = lane < TILE
        place = lax.rem(lane, TILE)

        def tile_count(r, c):
            a, b = (r + 1) // 2 - 1, (c + 1) // 2 - 1
            tile = (r + 1) % 2 * 2 + (c + 1) % 2
            return cnt[(a + 1) * 3 + b + 1, tile:tile + 1, :]

        for r in range(4):
            for pair in range(2):
                live = place < jnp.where(low, tile_count(r, 2 * pair), tile_count(r, 2 * pair + 1))
                for tile in range(4):
                    qr, qc = tile // 2, tile % 2
                    kr = r - qr
                    if not 0 <= kr < 3:
                        continue
                    picks = []
                    for c in (2 * pair, 2 * pair + 1):
                        e = c - qc
                        picks.append(mask_s[tile, 9 + 3 * kr + e] if 0 <= e < 3 else 0)
                    picked = jnp.where(low, picks[0], picks[1])
                    start = kr * 256 + pair * 128
                    bias[qr, qc:qc + 1, start:start + 128] = jnp.where(
                        live & (picked > 0), 0.0, NEG).astype(jnp.float32)

    def compute(head, qr):
        rows = pl.ds(pl.multiple_of(qr * 128, 128), 128)
        k = kv[head, 0, pl.ds(qr, 3)].reshape(768, HDIM)
        v = kv[head, 1, pl.ds(qr, 3)].reshape(768, HDIM)
        raw = lax.dot_general(qb[head, rows, :], k, (((1,), (1,)), ((), ())),
                              preferred_element_type=jnp.float32)
        raw = (raw.reshape(2, TILE, 768) + bias[qr].reshape(2, 1, 768)).reshape(128, 768)
        peak = jnp.max(raw, axis=1, keepdims=True)
        expo = jnp.exp2((raw - peak) * EXP_SCALE)
        total = jnp.sum(expo, axis=1, keepdims=True)
        summed = jnp.dot(expo.astype(jnp.bfloat16), v, preferred_element_type=jnp.float32)
        ob[head, rows, :] = (summed / total).astype(jnp.bfloat16)

    def give_back(head, part_row, first=0, last=HALF):
        def body(step, carry):
            peer = part_row * HALF + step

            @pl.when(peer != z)
            def _():
                pltpu.make_async_remote_copy(
                    src_ref=ob.at[head, rows_of(peer)],
                    dst_ref=out.at[:, columns(z, head)],
                    send_sem=out_send,
                    recv_sem=out_recv,
                    device_id=(blk, peer),
                    device_id_type=MESH,
                ).start()

            return carry

        lax.fori_loop(first, last, body, 0)

    scatter(0, 0, ALL)
    scatter(1, 0, ALL)
    send_counts()
    scatter(0, 1, ALL)
    scatter(1, 1, ALL)
    scatter(2, 0, ALL)
    scatter(0, 2, ALL)
    scatter(1, 2, ALL)
    for steps in (FAR, NEAR):
        for head in (1, 2):
            scatter(2, head, steps)

    def turn(i, carry):
        @pl.when(i < LOCAL_HEADS)
        def _():
            lax.fori_loop(0, 2, lambda array, carry: halo(array, i), None)

        @pl.when(i == 0)
        def _():
            build_bias()

        @pl.when(i > 0)
        def _():
            head = i - 1
            lax.fori_loop(0, 2, lambda array, carry: halo_arrived(array, head), None)
            wait_bytes(qb.at[head], in_recv.at[head, 2])
            first = jnp.where(head == 1, core, 0)

            few = jnp.where((head == 1) & (core == 0), 3, HALF)

            def attend(row):
                compute(head, row)
                give_back(head, row, 0, few)

            attend(first)
            pl.when((head == 0) | ((head == 1) & (core == 1)))(lambda: attend(1 - first))

        return carry

    lax.fori_loop(0, LOCAL_HEADS + 1, turn, 0)

    @pl.when(core == 0)
    def _():
        give_back(1, 0, 3, HALF)
        compute(1, 1)
        give_back(1, 1)
        compute(2, 1)
        give_back(2, 1)

    @pl.when(core == 1)
    def _():
        compute(2, 1)
        give_back(2, 1)

    for head in range(LOCAL_HEADS):
        pltpu.make_async_copy(ob.at[head, rows_of(z)], out.at[:, columns(z, head)], out_recv).start()

    sent = pl.ds(0, LOCAL_HEADS * (ULY - 1) * HDIM)
    for array in range(3):
        wait_bytes(sources[array].at[:, sent], send_sem.at[array])
    for a, b in others:
        @if_inside(a, b)
        def _():
            index = (a + 1) * 3 + b + 1
            wait_bytes(kv.at[:, :, near(a), near(b)], halo_send.at[index])
            wait_bytes(cnt.at[4], cnt_send.at[index])
    wait_bytes(out.at[:, sent], out_send)
    wait_bytes(out, out_recv)


def on_device(queries, keys, values, window_mask, valid_count):
    heads = LOCAL_HEADS
    dma = pltpu.SemaphoreType.DMA
    return pl.pallas_call(
        kernel,
        out_shape=jax.ShapeDtypeStruct(queries.shape, queries.dtype),
        in_specs=[pl.BlockSpec(memory_space=pl.ANY)] * 5,
        out_specs=pl.BlockSpec(memory_space=pltpu.VMEM),
        scratch_shapes=[
            pltpu.VMEM((heads, 2, 4, 4, TILE, HDIM), jnp.bfloat16),
            pltpu.VMEM((heads, 256, HDIM), jnp.bfloat16),
            pltpu.VMEM((heads, 256, HDIM), jnp.bfloat16),
            pltpu.VMEM((9, 8, 128), jnp.int32),
            pltpu.VMEM((2, 2, 768), jnp.float32),
            pltpu.SMEM((4,), jnp.int32),
            pltpu.SMEM((4, 27), jnp.int32),
            dma((2,)), dma((3,)), dma((9,)), dma((9,)), dma,
            dma((heads, 3)), dma((heads, 2, 9)), dma((9,)), dma,
            pltpu.VMEM((3,) + queries.shape, jnp.bfloat16), dma((3,)),
        ],
        compiler_params=pltpu.CompilerParams(
            collective_id=0, has_side_effects=True, vmem_limit_bytes=56 * 1024 * 1024),
    )(valid_count, window_mask, queries, keys, values)


def solution(mesh):
    in_specs = (
        P(("blk", "uly"), None),
        P(("blk", "uly"), None),
        P(("blk", "uly"), None),
        P("blk", None),
        P("blk"),
    )
    out_specs = P(("blk", "uly"), None)
    return jax.shard_map(
        on_device, mesh=mesh, in_specs=in_specs, out_specs=out_specs, check_vma=False
    )
```
